32 devices in a mesh: groups: 2 (over x), dp: 16 (over z, y, core).
Axes of the slice: x: 2, y: 2, z: 4, core: 2. Of those that a mesh axis runs over, the one named last changes fastest.
Arguments:
- embeddings: bfloat16 [96, 512, 256], P(('groups', 'dp')), parts along dimension 0, may hold values from -6 to 6
- projection: bfloat16 [512, 64], replicated, may hold values from -0.25 to 0.25
- norm_gain: float32 [16384], replicated, may hold values from 0.5 to 1.5
- norm_bias: float32 [16384], replicated, may hold values from -3 to 3
- up_weight: bfloat16 [16384, 4096], P('dp'), may hold values from -0.046875 to 0.046875
- up_bias: float32 [4096], replicated, may hold values from -3 to 3
- down_weight: bfloat16 [4096, 16384], P(None, 'dp'), may hold values from -0.09375 to 0.09375
- cotangent: bfloat16 [96, 16384], P('groups', 'dp'), parts along dimension 0, may hold values from -0.59765625 to 0.59765625
Outputs:
- interaction_out: bfloat16 [96, 16384], P('groups', 'dp'), parts along dimension 0
- grad_embeddings: bfloat16 [96, 512, 256], P(('groups', 'dp')), parts along dimension 0
- grad_projection: float32 [1024, 64], P('groups'), parts along dimension 0
- grad_gain: float32 [32768], P('groups'), parts along dimension 0
- grad_bias: float32 [32768], P('groups'), parts along dimension 0
- grad_up: float32 [32768, 4096], P(('groups', 'dp')), parts along dimension 0
- grad_up_bias: float32 [8192], P('groups'), parts along dimension 0
- grad_down: float32 [8192, 16384], P('groups', 'dp'), parts along dimension 0
The draws below stay inside these ranges and needn't reach their ends.
There are 2 independent parts, one for each index of `groups`. The reference program is written for one: setup_inputs(seed, part) draws one part's arguments, and reference() takes and returns one part's arrays. A program takes and returns all parts, laid end to end along the dimension named above; an argument that names none is the same for every part. Nothing has to cross between parts.
All inputs are finite; a program needn't handle non-finite values.
Results may differ from the reference program's by a relative error of at most 0.01.
Values may be sent and summed in bfloat16 or wider, within the bound.
A program may use at most 128 MiB of HBM per device.

```python
import jax
import jax.numpy as jnp
from jax import lax

N_EMB = 512
D = 256
K = 64
HID = 4096
F_IN = 16384
ROWS = 48


def steps_of(rng, extent, shards, least, largest):
    factor_of = 1.0
    for position, parts in shards:
        steps = jax.random.uniform(jax.random.fold_in(jax.random.fold_in(rng, 6), position), (parts,), jnp.float32, least / len(shards), largest / len(shards))
        factor_of = factor_of * jnp.repeat(jnp.exp(steps), extent[position] // parts).reshape((-1,) + (1,) * (len(extent) - 1 - position))
    return factor_of


def scatter_about(stream_key, extent, width, reach, shards=(), kind=jnp.bfloat16):
    entries = jax.random.normal(stream_key, extent, jnp.float32) * width
    if len(shards) > 0:
        entries = steps_of(stream_key, extent, shards, -0.22, 0.18) * entries
    return jnp.clip(entries, min=-reach, max=reach).astype(kind)


def setup_inputs(seed: int = 0, part: int = 0) -> dict:
    seeds = jax.random.split(jax.random.key(seed), 9)
    part_splits = jax.random.split(jax.random.fold_in(seeds[8], part), 9)
    return {
        "embeddings": scatter_about(part_splits[0], (ROWS, N_EMB, D), 1.0, 6.0, ((0, 16),)),
        "projection": scatter_about(seeds[1], (N_EMB, K), N_EMB ** -0.5, 0.25),
        "norm_gain": jnp.clip(1.0 + 0.1 * jax.random.normal(seeds[2], (F_IN,), jnp.float32), 0.5, 1.5),
        "norm_bias": scatter_about(seeds[3], (F_IN,), 0.5, 3.0, (), jnp.float32),
        "up_weight": scatter_about(seeds[4], (F_IN, HID), F_IN ** -0.5, 0.046875, ((0, 16),)),
        "up_bias": scatter_about(seeds[5], (HID,), 0.5, 3.0, (), jnp.float32),
        "down_weight": scatter_about(seeds[6], (HID, F_IN), HID ** -0.5, 0.09375, ((1, 16),)),
        "cotangent": scatter_about(part_splits[7], (ROWS, F_IN), 0.1, 0.59765625, ((1, 16),)),
    }


epsilon = 1e-05

def activate(values):
    return jax.nn.gelu(values, approximate=True)

def activate_back(preact, grad_hidden):
    _, pullback = jax.vjp(activate, preact)
    return pullback(grad_hidden)[0]

def interact_row(sample, projection):
    pair_dots = jnp.dot(sample, sample.T, preferred_element_type=jnp.float32).astype(jnp.bfloat16)
    compressed = jnp.dot(pair_dots, projection, preferred_element_type=jnp.float32).astype(jnp.bfloat16)
    interaction = jnp.dot(sample.T, compressed, preferred_element_type=jnp.float32)
    return interaction.reshape(-1)

def interact_back(sample, projection, grad_flat):
    pair_dots = jnp.dot(sample, sample.T, preferred_element_type=jnp.float32).astype(jnp.bfloat16)
    compressed = jnp.dot(pair_dots, projection, preferred_element_type=jnp.float32).astype(jnp.bfloat16)
    grad_matrix = grad_flat.reshape(sample.shape[1], projection.shape[1])
    grad_compressed = jnp.dot(sample, grad_matrix, preferred_element_type=jnp.float32).astype(jnp.bfloat16)
    grad_direct = jnp.dot(compressed, grad_matrix.T, preferred_element_type=jnp.float32)
    grad_pairs = jnp.dot(grad_compressed, projection.T, preferred_element_type=jnp.float32).astype(jnp.bfloat16)
    grad_sample = grad_direct + jnp.dot(grad_pairs, sample, preferred_element_type=jnp.float32)
    grad_sample = grad_sample + jnp.dot(grad_pairs.T, sample, preferred_element_type=jnp.float32)
    grad_proj = jnp.dot(pair_dots.T, grad_compressed, preferred_element_type=jnp.float32)
    return (grad_sample.astype(jnp.bfloat16), grad_proj)

def layer_norm(interaction):
    centre = interaction - lax.optimization_barrier(jnp.mean(interaction, axis=-1, keepdims=True))
    variance = lax.optimization_barrier(jnp.mean(centre * centre, axis=-1, keepdims=True))
    inv_scale = lax.rsqrt(variance + epsilon)
    return (centre * inv_scale, inv_scale)

def norm_back(grad_normed, standard, inv_scale, norm_gain):
    scaled = grad_normed * norm_gain
    first = lax.optimization_barrier(jnp.mean(scaled, axis=-1, keepdims=True))
    second = lax.optimization_barrier(jnp.mean(scaled * standard, axis=-1, keepdims=True))
    return inv_scale * (scaled - first - standard * second)

def reference(embeddings, projection, norm_gain, norm_bias, up_weight, up_bias, down_weight, cotangent):
    interaction = lax.map(lambda sample: interact_row(sample, projection), embeddings)
    standard, inv_scale = layer_norm(interaction)
    normed = (standard * norm_gain + norm_bias).astype(jnp.bfloat16)
    preact = jnp.dot(normed, up_weight, preferred_element_type=jnp.float32) + up_bias
    hidden = activate(preact).astype(jnp.bfloat16)
    interaction_out = jnp.dot(hidden, down_weight, preferred_element_type=jnp.float32).astype(jnp.bfloat16)
    grad_hidden = jnp.dot(cotangent, down_weight.T, preferred_element_type=jnp.float32)
    grad_preact = activate_back(preact, grad_hidden).astype(jnp.bfloat16)
    grad_down = jnp.dot(hidden.T, cotangent, preferred_element_type=jnp.float32)
    grad_up = jnp.dot(normed.T, grad_preact, preferred_element_type=jnp.float32)
    grad_up_bias = lax.optimization_barrier(jnp.sum(grad_preact.astype(jnp.float32), axis=0))
    grad_normed = jnp.dot(grad_preact, up_weight.T, preferred_element_type=jnp.float32).astype(jnp.bfloat16)
    grad_normed = grad_normed.astype(jnp.float32)
    grad_gain = lax.optimization_barrier(jnp.sum(grad_normed * standard, axis=0))
    grad_bias = lax.optimization_barrier(jnp.sum(grad_normed, axis=0))
    grad_interaction = norm_back(grad_normed, standard, inv_scale, norm_gain).astype(jnp.bfloat16)

    def per_row(running, inputs):
        sample, grad_flat = inputs
        grad_sample, grad_proj = interact_back(sample, projection, grad_flat)
        return (running + grad_proj, grad_sample)
    start_proj = jnp.zeros(projection.shape, jnp.float32)
    grad_projection, grad_embeddings = lax.scan(per_row, start_proj, (embeddings, grad_interaction))
    return (interaction_out, grad_embeddings, grad_projection, grad_gain, grad_bias, grad_up, grad_up_bias, grad_down)
```

```python
import functools
import math

import jax
import jax.numpy as jnp
from jax import lax
from jax.experimental import pallas as pl
from jax.experimental.pallas import tpu as pltpu
from jax.sharding import PartitionSpec as P

epsilon = 1e-05


def activate(values):
    return jax.nn.gelu(values, approximate=True)


def activate_back(preact, grad_hidden):
    _, pullback = jax.vjp(activate, preact)
    return pullback(grad_hidden)[0]


def interact_row(sample, projection):
    pair_dots = jnp.dot(sample, sample.T, preferred_element_type=jnp.float32).astype(jnp.bfloat16)
    compressed = jnp.dot(pair_dots, projection, preferred_element_type=jnp.float32).astype(
        jnp.bfloat16
    )
    interaction = jnp.dot(sample.T, compressed, preferred_element_type=jnp.float32)
    return interaction.reshape(-1)


def interact_back(sample, projection, grad_flat):
    pair_dots = jnp.dot(sample, sample.T, preferred_element_type=jnp.float32).astype(jnp.bfloat16)
    compressed = jnp.dot(pair_dots, projection, preferred_element_type=jnp.float32).astype(
        jnp.bfloat16
    )
    grad_matrix = grad_flat.reshape(sample.shape[1], projection.shape[1])
    grad_compressed = jnp.dot(sample, grad_matrix, preferred_element_type=jnp.float32).astype(
        jnp.bfloat16
    )
    grad_direct = jnp.dot(compressed, grad_matrix.T, preferred_element_type=jnp.float32)
    grad_pairs = jnp.dot(grad_compressed, projection.T, preferred_element_type=jnp.float32).astype(
        jnp.bfloat16
    )
    grad_sample = grad_direct + jnp.dot(grad_pairs, sample, preferred_element_type=jnp.float32)
    grad_sample = grad_sample + jnp.dot(grad_pairs.T, sample, preferred_element_type=jnp.float32)
    grad_proj = jnp.dot(pair_dots.T, grad_compressed, preferred_element_type=jnp.float32)
    return (grad_sample.astype(jnp.bfloat16), grad_proj)


def layer_norm(interaction):
    centre = interaction - jnp.mean(interaction, axis=-1, keepdims=True)
    variance = jnp.mean(centre * centre, axis=-1, keepdims=True)
    inv_scale = lax.rsqrt(variance + epsilon)
    return (centre * inv_scale, inv_scale)


def norm_back(grad_normed, standard, inv_scale, norm_gain):
    scaled = grad_normed * norm_gain
    first = jnp.mean(scaled, axis=-1, keepdims=True)
    second = jnp.mean(scaled * standard, axis=-1, keepdims=True)
    return inv_scale * (scaled - first - standard * second)


def sum_rows(term, own_rows):
    return lax.psum_scatter(
        term(jnp.int32(0), lax.axis_size("dp") * own_rows), "dp", scatter_dimension=0, tiled=True
    )


def fold_rows(values, step_fn, initial):
    return step_fn(initial, lax.all_gather(values, "dp", axis=0, tiled=True), jnp.int32(0))


def contract_rows(left, right):
    return lax.dot_general(
        left, right, (((0,), (0,)), ((), ())), preferred_element_type=jnp.float32
    )


def contract_last(left, right):
    return lax.dot_general(
        left, right, (((1,), (1,)), ((), ())), preferred_element_type=jnp.float32
    )


def plain_body(embeddings, projection, norm_gain, norm_bias, up_weight, up_bias, down_weight, cotangent):
    own_rows = embeddings.shape[0]
    interaction = jax.vmap(lambda sample: interact_row(sample, projection))(embeddings)
    standard, inv_scale = layer_norm(interaction)
    normed = (standard * norm_gain + norm_bias).astype(jnp.bfloat16)
    columns = lax.all_to_all(normed, "dp", split_axis=1, concat_axis=0, tiled=True)
    all_rows = columns.shape[0]
    own_features = up_weight.shape[0]
    hidden_units = up_weight.shape[1]

    def preact_term(offset, amount):
        return jnp.dot(columns, up_weight, preferred_element_type=jnp.float32)

    preact = sum_rows(preact_term, own_rows) + up_bias
    hidden = activate(preact).astype(jnp.bfloat16)

    def output_step(running, block_rows, offset):
        product = jnp.dot(block_rows, down_weight, preferred_element_type=jnp.float32)
        down_acc = contract_rows(block_rows, cotangent)
        return (product, down_acc)

    start_state = (
        jnp.zeros((all_rows, down_weight.shape[1]), jnp.float32),
        jnp.zeros(down_weight.shape, jnp.float32),
    )
    out_columns, grad_down = fold_rows(hidden, output_step, start_state)

    def hidden_term(offset, amount):
        return contract_last(cotangent, down_weight)

    grad_hidden = sum_rows(hidden_term, own_rows)
    grad_preact = activate_back(preact, grad_hidden).astype(jnp.bfloat16)

    def gradient_step(running, block_rows, offset):
        product = contract_last(block_rows, up_weight)
        up_acc = contract_rows(columns, block_rows)
        bias_acc = jnp.sum(block_rows.astype(jnp.float32), axis=0)
        return (product, up_acc, bias_acc)

    start_grad = (
        jnp.zeros((all_rows, own_features), jnp.float32),
        jnp.zeros(up_weight.shape, jnp.float32),
        jnp.zeros((hidden_units,), jnp.float32),
    )
    back_columns, grad_up, grad_up_bias = fold_rows(grad_preact, gradient_step, start_grad)
    grad_normed = lax.all_to_all(
        back_columns.astype(jnp.bfloat16), "dp", split_axis=0, concat_axis=1, tiled=True
    ).astype(jnp.float32)
    gain_part = jnp.sum(grad_normed * standard, axis=0)
    bias_part = jnp.sum(grad_normed, axis=0)
    grad_interaction = norm_back(grad_normed, standard, inv_scale, norm_gain).astype(jnp.bfloat16)
    grad_embeddings, proj_rows = jax.vmap(
        lambda sample, grad_flat: interact_back(sample, projection, grad_flat)
    )(embeddings, grad_interaction)
    proj_part = jnp.sum(proj_rows, axis=0)
    grad_projection, grad_gain, grad_bias = lax.psum((proj_part, gain_part, bias_part), "dp")
    return (
        out_columns.astype(jnp.bfloat16),
        grad_embeddings,
        grad_projection,
        grad_gain,
        grad_bias,
        grad_up,
        grad_up_bias,
        grad_down,
    )


MESH = pl.DeviceIdType.MESH


def greet(n, me):
    barrier = pltpu.get_barrier_semaphore()

    def signal(step, carry):
        peer = lax.rem(me + step, n)
        pl.semaphore_signal(barrier, inc=1, device_id={"dp": peer}, device_id_type=MESH)
        return carry

    lax.fori_loop(1, n, signal, 0)
    pl.semaphore_wait(barrier, n - 1)


def remote(source, target, sent, arrived, peer):
    return pltpu.make_async_remote_copy(
        src_ref=source,
        dst_ref=target,
        send_sem=sent,
        recv_sem=arrived,
        device_id={"dp": peer},
        device_id_type=MESH,
    )


class Exchange:
    def __init__(self, n, me, source, target, sent, arrived, same=False):
        self.n, self.me, self.source, self.target = n, me, source, target
        self.sent, self.arrived, self.same = sent, arrived, same

    def copy(self, peer, slot):
        source = self.source if self.same else self.source.at[peer]
        return remote(
            source, self.target.at[slot], self.sent.at[peer], self.arrived.at[slot], peer
        )

    def send(self, peer):
        self.copy(peer, self.me).start()

    def receive(self, peer):
        self.copy(peer, peer).wait_recv()

    def each(self, step_fn):
        def step(k, carry):
            step_fn(lax.rem(self.me + k, self.n))
            return carry

        lax.fori_loop(1, self.n, step, 0)

    def send_all(self):
        self.each(self.send)

    def receive_all(self):
        self.each(lambda peer: self.receive(lax.rem(2 * self.me + self.n - peer, self.n)))

    def finish(self):
        self.each(lambda peer: self.copy(peer, self.me).wait_send())


def mlp_kernel(
    n,
    standard_ref,
    gain_ref,
    bias_ref,
    up_bias_ref,
    cot_ref,
    up_hbm,
    down_hbm,
    out_ref,
    columns_ref,
    hidden_ref,
    grad_preact_ref,
    up_bias_grad_ref,
    back_ref,
    sums_ref,
    up_ref,
    down_ref,
    std_in,
    std_rows,
    gh_send,
    gh_recv,
    pre_send,
    pre_recv,
    act_all,
    back_send,
    sums_own,
    out_acc,
    back_acc,
    up_sem,
    down_sem,
    std_ss,
    std_rs,
    gh_ss,
    gh_rs,
    pre_ss,
    pre_rs,
    act_ss,
    act_rs,
    back_ss,
    back_rs,
    sums_ss,
    sums_rs,
):
    me = lax.axis_index("dp")
    own = standard_ref.shape[1]
    rows = cot_ref.shape[0]
    width = up_ref.shape[2]

    def up_copy(j):
        start = pl.multiple_of(j * width, width)
        return pltpu.make_async_copy(up_hbm.at[:, pl.ds(start, width)], up_ref.at[j], up_sem.at[j])

    def down_copy(j):
        start = pl.multiple_of(j * width, width)
        return pltpu.make_async_copy(
            down_hbm.at[pl.ds(start, width), :], down_ref.at[j], down_sem.at[j]
        )

    def loop(step_fn):
        def step(k, carry):
            step_fn(lax.rem(me + k, n))
            return carry

        lax.fori_loop(1, n + 1, step, 0)

    loop(lambda j: down_copy(j).start())
    loop(lambda j: up_copy(j).start())
    greet(n, me)

    std = Exchange(n, me, standard_ref, std_in, std_ss, std_rs)
    gh = Exchange(n, me, gh_send, gh_recv, gh_ss, gh_rs)
    pre = Exchange(n, me, pre_send, pre_recv, pre_ss, pre_rs)
    act = Exchange(n, me, act_all.at[me], act_all, act_ss, act_rs, same=True)
    back = Exchange(n, me, back_send, back_ref, back_ss, back_rs)
    sums = Exchange(n, me, sums_own, sums_ref, sums_ss, sums_rs, same=True)

    std.send_all()
    std_in[me] = standard_ref[me]

    def hidden_step(j):
        down_copy(j).wait()
        part = lax.dot_general(
            cot_ref[...], down_ref[j], (((1,), (1,)), ((), ())), preferred_element_type=jnp.float32
        ).astype(jnp.bfloat16)

        @pl.when(j != me)
        def _():
            gh_send[j] = part
            gh.send(j)

        @pl.when(j == me)
        def _():
            gh_recv[me] = part

    loop(hidden_step)

    std.receive_all()
    for j in range(n):
        std_rows[own * j : own * (j + 1), :] = std_in[j].astype(jnp.float32)
    columns_ref[...] = (std_rows[...] * gain_ref[me] + bias_ref[me]).astype(jnp.bfloat16)

    def preact_step(j):
        up_copy(j).wait()
        part = jnp.dot(
            columns_ref[...], up_ref[j], preferred_element_type=jnp.float32
        ).astype(jnp.bfloat16)

        @pl.when(j != me)
        def _():
            pre_send[j] = part
            pre.send(j)

        @pl.when(j == me)
        def _():
            pre_recv[me] = part

    loop(preact_step)

    gh.receive_all()
    grad_hidden = gh_recv[0].astype(jnp.float32)
    for j in range(1, n):
        grad_hidden = grad_hidden + gh_recv[j].astype(jnp.float32)
    pre.receive_all()
    preact = pre_recv[0].astype(jnp.float32)
    for j in range(1, n):
        preact = preact + pre_recv[j].astype(jnp.float32)
    preact = preact + up_bias_ref[me]
    root = math.sqrt(2 / math.pi)
    square = preact * preact
    bent = jnp.tanh(root * preact * (1.0 + 0.044715 * square))
    half = 0.5 * (1.0 + bent)
    slope = half + 0.5 * preact * (1.0 - bent * bent) * (root * (1.0 + 3 * 0.044715 * square))
    act_all[me, 0] = (preact * half).astype(jnp.bfloat16)
    act_all[me, 1] = (grad_hidden * slope).astype(jnp.bfloat16)
    act.send_all()

    def gather_step(j):
        columns = pl.ds(pl.multiple_of(j * width, width), width)
        hidden = act_all[j, 0]
        grad = act_all[j, 1]
        hidden_ref[:, columns] = hidden
        grad_preact_ref[:, columns] = grad
        up_bias_grad_ref[:, columns] = jnp.sum(grad.astype(jnp.float32), axis=0, keepdims=True)
        out_acc[...] += jnp.dot(hidden, down_ref[j], preferred_element_type=jnp.float32)
        back_acc[...] += lax.dot_general(
            grad, up_ref[j], (((1,), (1,)), ((), ())), preferred_element_type=jnp.float32
        )

    out_acc[...] = jnp.zeros_like(out_acc)
    back_acc[...] = jnp.zeros_like(back_acc)
    gather_step(me)

    def arrive_step(k, carry):
        j = lax.rem(me + n - k, n)
        act.receive(j)
        gather_step(j)
        return carry

    lax.fori_loop(1, n, arrive_step, 0)

    grad_normed = back_acc[...].astype(jnp.bfloat16)
    wide = grad_normed.astype(jnp.float32)
    back_acc[...] = wide
    for j in range(n):
        back_send[j] = back_acc[own * j : own * (j + 1), :].astype(jnp.bfloat16)
    back.send_all()
    back_ref[me] = back_send[me]
    sums_own[0:1, :] = jnp.sum(wide * std_rows[...], axis=0, keepdims=True)
    sums_own[1:2, :] = jnp.sum(wide, axis=0, keepdims=True)
    sums.send_all()
    sums_ref[me] = sums_own[...]
    out_ref[...] = out_acc[...].astype(jnp.bfloat16)
    for exchange in (std, gh, pre, act):
        exchange.finish()
    back.receive_all()
    sums.receive_all()
    back.finish()
    sums.finish()


def mlp(standard, norm_gain, norm_bias, up_weight, up_bias, down_weight, cotangent):
    n = lax.axis_size("dp")
    own = standard.shape[0]
    rows, features = cotangent.shape
    units = up_weight.shape[1]
    width = units // n
    blocks = jnp.swapaxes(standard.astype(jnp.bfloat16).reshape(own, n, features), 0, 1)
    vmem = pl.BlockSpec(memory_space=pltpu.VMEM)
    hbm = pl.BlockSpec(memory_space=pl.ANY)
    bf16, f32 = jnp.bfloat16, jnp.float32
    shape = jax.ShapeDtypeStruct
    return pl.pallas_call(
        functools.partial(mlp_kernel, n),
        out_shape=(
            shape((rows, features), bf16),
            shape((rows, features), bf16),
            shape((rows, units), bf16),
            shape((rows, units), bf16),
            shape((1, units), f32),
            shape((n, own, features), bf16),
            shape((n, 2, features), f32),
        ),
        in_specs=[vmem] * 5 + [hbm] * 2,
        out_specs=[vmem] * 7,
        scratch_shapes=[
            pltpu.VMEM((n, features, width), bf16),
            pltpu.VMEM((n, width, features), bf16),
            pltpu.VMEM((n, own, features), bf16),
            pltpu.VMEM((rows, features), f32),
            pltpu.VMEM((n, rows, width), bf16),
            pltpu.VMEM((n, rows, width), bf16),
            pltpu.VMEM((n, rows, width), bf16),
            pltpu.VMEM((n, rows, width), bf16),
            pltpu.VMEM((n, 2, rows, width), bf16),
            pltpu.VMEM((n, own, features), bf16),
            pltpu.VMEM((2, features), f32),
            pltpu.VMEM((rows, features), f32),
            pltpu.VMEM((rows, features), f32),
        ]
        + [pltpu.SemaphoreType.DMA((n,))] * 14,
        compiler_params=pltpu.CompilerParams(
            collective_id=0, has_side_effects=True, vmem_limit_bytes=48 * 2**20
        ),
        cost_estimate=pl.CostEstimate(
            flops=8 * rows * features * units,
            bytes_accessed=4 * features * units,
            transcendentals=rows * width,
        ),
        name="perceptron",
    )(
        blocks,
        norm_gain.reshape(n, 1, features),
        norm_bias.reshape(n, 1, features),
        up_bias.reshape(n, 1, width),
        cotangent,
        up_weight,
        down_weight,
    )


def total_kernel(n, part_ref, total_ref, parts, own_total, part_ss, part_rs, total_ss, total_rs):
    me = lax.axis_index("dp")
    greet(n, me)
    first = Exchange(n, me, part_ref, parts, part_ss, part_rs)
    second = Exchange(n, me, own_total, total_ref, total_ss, total_rs, same=True)
    first.send_all()
    parts[me] = part_ref[me]
    first.receive_all()
    total = parts[0]
    for j in range(1, n):
        total = total + parts[j]
    own_total[...] = total
    second.send_all()
    total_ref[me] = total
    first.finish()
    second.receive_all()
    second.finish()


def total_over_rows(part):
    n = lax.axis_size("dp")
    height, width = part.shape
    vmem = pl.BlockSpec(memory_space=pltpu.VMEM)
    blocks = (n, height // n, width)
    total = pl.pallas_call(
        functools.partial(total_kernel, n),
        out_shape=jax.ShapeDtypeStruct(blocks, jnp.float32),
        in_specs=[vmem],
        out_specs=vmem,
        scratch_shapes=[
            pltpu.VMEM(blocks, jnp.float32),
            pltpu.VMEM(blocks[1:], jnp.float32),
        ]
        + [pltpu.SemaphoreType.DMA((n,))] * 4,
        compiler_params=pltpu.CompilerParams(collective_id=1, has_side_effects=True),
        name="total",
    )(part.reshape(blocks))
    return total.reshape(height, width)


def body(embeddings, projection, norm_gain, norm_bias, up_weight, up_bias, down_weight, cotangent):
    n = lax.axis_size("dp")
    own_rows = embeddings.shape[0]
    if (up_weight.shape[1] // n) % 128 or cotangent.shape[0] % 16:
        return plain_body(
            embeddings, projection, norm_gain, norm_bias, up_weight, up_bias, down_weight, cotangent
        )
    interaction = jax.vmap(lambda sample: interact_row(sample, projection))(embeddings)
    standard, inv_scale = layer_norm(interaction)
    out, columns, hidden, grad_preact, grad_up_bias, back, sums = mlp(
        standard, norm_gain, norm_bias, up_weight, up_bias, down_weight, cotangent
    )
    grad_up = contract_rows(columns, grad_preact)
    grad_down = contract_rows(hidden, cotangent)
    grad_normed = jnp.swapaxes(back, 0, 1).reshape(own_rows, -1).astype(jnp.float32)
    grad_interaction = norm_back(grad_normed, standard, inv_scale, norm_gain).astype(jnp.bfloat16)
    grad_embeddings, proj_rows = jax.vmap(
        lambda sample, grad_flat: interact_back(sample, projection, grad_flat)
    )(embeddings, grad_interaction)
    grad_projection = total_over_rows(jnp.sum(proj_rows, axis=0))
    return (
        out,
        grad_embeddings,
        grad_projection,
        sums[:, 0, :].reshape(-1),
        sums[:, 1, :].reshape(-1),
        grad_up,
        grad_up_bias.reshape(-1),
        grad_down,
    )


def solution(mesh):
    return jax.shard_map(
        body,
        mesh=mesh,
        in_specs=(
            P(("groups", "dp"), None, None),
            P(),
            P(),
            P(),
            P("dp", None),
            P(),
            P(None, "dp"),
            P("groups", "dp"),
        ),
        out_specs=(
            P("groups", "dp"),
            P(("groups", "dp"), None, None),
            P("groups", None),
            P("groups"),
            P("groups"),
            P(("groups", "dp"), None),
            P("groups"),
            P("groups", "dp"),
        ),
        check_vma=False,
    )
```

```python
import functools
import math

import jax
import jax.numpy as jnp
from jax import lax
from jax.experimental import pallas as pl
from jax.experimental.pallas import tpu as pltpu
from jax.sharding import PartitionSpec as P

epsilon = 1e-05


def activate(values):
    return jax.nn.gelu(values, approximate=True)


def activate_back(preact, grad_hidden):
    _, pullback = jax.vjp(activate, preact)
    return pullback(grad_hidden)[0]


def interact_row(sample, projection):
    pair_dots = jnp.dot(sample, sample.T, preferred_element_type=jnp.float32).astype(jnp.bfloat16)
    compressed = jnp.dot(pair_dots, projection, preferred_element_type=jnp.float32).astype(
        jnp.bfloat16
    )
    interaction = jnp.dot(sample.T, compressed, preferred_element_type=jnp.float32)
    return interaction.reshape(-1)


def interact_back(sample, projection, grad_flat):
    pair_dots = jnp.dot(sample, sample.T, preferred_element_type=jnp.float32).astype(jnp.bfloat16)
    compressed = jnp.dot(pair_dots, projection, preferred_element_type=jnp.float32).astype(
        jnp.bfloat16
    )
    grad_matrix = grad_flat.reshape(sample.shape[1], projection.shape[1])
    grad_compressed = jnp.dot(sample, grad_matrix, preferred_element_type=jnp.float32).astype(
        jnp.bfloat16
    )
    grad_direct = jnp.dot(compressed, grad_matrix.T, preferred_element_type=jnp.float32)
    grad_pairs = jnp.dot(grad_compressed, projection.T, preferred_element_type=jnp.float32).astype(
        jnp.bfloat16
    )
    grad_sample = grad_direct + jnp.dot(grad_pairs, sample, preferred_element_type=jnp.float32)
    grad_sample = grad_sample + jnp.dot(grad_pairs.T, sample, preferred_element_type=jnp.float32)
    grad_proj = jnp.dot(pair_dots.T, grad_compressed, preferred_element_type=jnp.float32)
    return (grad_sample.astype(jnp.bfloat16), grad_proj)


def layer_norm(interaction):
    centre = interaction - jnp.mean(interaction, axis=-1, keepdims=True)
    variance = jnp.mean(centre * centre, axis=-1, keepdims=True)
    inv_scale = lax.rsqrt(variance + epsilon)
    return (centre * inv_scale, inv_scale)


def norm_back(grad_normed, standard, inv_scale, norm_gain):
    scaled = grad_normed * norm_gain
    first = jnp.mean(scaled, axis=-1, keepdims=True)
    second = jnp.mean(scaled * standard, axis=-1, keepdims=True)
    return inv_scale * (scaled - first - standard * second)


def sum_rows(term, own_rows):
    return lax.psum_scatter(
        term(jnp.int32(0), lax.axis_size("dp") * own_rows), "dp", scatter_dimension=0, tiled=True
    )


def fold_rows(values, step_fn, initial):
    return step_fn(initial, lax.all_gather(values, "dp", axis=0, tiled=True), jnp.int32(0))


def contract_rows(left, right):
    return lax.dot_general(
        left, right, (((0,), (0,)), ((), ())), preferred_element_type=jnp.float32
    )


def contract_last(left, right):
    return lax.dot_general(
        left, right, (((1,), (1,)), ((), ())), preferred_element_type=jnp.float32
    )


def plain_body(embeddings, projection, norm_gain, norm_bias, up_weight, up_bias, down_weight, cotangent):
    own_rows = embeddings.shape[0]
    interaction = jax.vmap(lambda sample: interact_row(sample, projection))(embeddings)
    standard, inv_scale = layer_norm(interaction)
    normed = (standard * norm_gain + norm_bias).astype(jnp.bfloat16)
    columns = lax.all_to_all(normed, "dp", split_axis=1, concat_axis=0, tiled=True)
    all_rows = columns.shape[0]
    own_features = up_weight.shape[0]
    hidden_units = up_weight.shape[1]

    def preact_term(offset, amount):
        return jnp.dot(columns, up_weight, preferred_element_type=jnp.float32)

    preact = sum_rows(preact_term, own_rows) + up_bias
    hidden = activate(preact).astype(jnp.bfloat16)

    def output_step(running, block_rows, offset):
        product = jnp.dot(block_rows, down_weight, preferred_element_type=jnp.float32)
        down_acc = contract_rows(block_rows, cotangent)
        return (product, down_acc)

    start_state = (
        jnp.zeros((all_rows, down_weight.shape[1]), jnp.float32),
        jnp.zeros(down_weight.shape, jnp.float32),
    )
    out_columns, grad_down = fold_rows(hidden, output_step, start_state)

    def hidden_term(offset, amount):
        return contract_last(cotangent, down_weight)

    grad_hidden = sum_rows(hidden_term, own_rows)
    grad_preact = activate_back(preact, grad_hidden).astype(jnp.bfloat16)

    def gradient_step(running, block_rows, offset):
        product = contract_last(block_rows, up_weight)
        up_acc = contract_rows(columns, block_rows)
        bias_acc = jnp.sum(block_rows.astype(jnp.float32), axis=0)
        return (product, up_acc, bias_acc)

    start_grad = (
        jnp.zeros((all_rows, own_features), jnp.float32),
        jnp.zeros(up_weight.shape, jnp.float32),
        jnp.zeros((hidden_units,), jnp.float32),
    )
    back_columns, grad_up, grad_up_bias = fold_rows(grad_preact, gradient_step, start_grad)
    grad_normed = lax.all_to_all(
        back_columns.astype(jnp.bfloat16), "dp", split_axis=0, concat_axis=1, tiled=True
    ).astype(jnp.float32)
    gain_part = jnp.sum(grad_normed * standard, axis=0)
    bias_part = jnp.sum(grad_normed, axis=0)
    grad_interaction = norm_back(grad_normed, standard, inv_scale, norm_gain).astype(jnp.bfloat16)
    grad_embeddings, proj_rows = jax.vmap(
        lambda sample, grad_flat: interact_back(sample, projection, grad_flat)
    )(embeddings, grad_interaction)
    proj_part = jnp.sum(proj_rows, axis=0)
    grad_projection, grad_gain, grad_bias = lax.psum((proj_part, gain_part, bias_part), "dp")
    return (
        out_columns.astype(jnp.bfloat16),
        grad_embeddings,
        grad_projection,
        grad_gain,
        grad_bias,
        grad_up,
        grad_up_bias,
        grad_down,
    )


MESH = pl.DeviceIdType.MESH


def greet(n, me):
    barrier = pltpu.get_barrier_semaphore()

    def signal(step, carry):
        peer = lax.rem(me + step, n)
        pl.semaphore_signal(barrier, inc=1, device_id={"dp": peer}, device_id_type=MESH)
        return carry

    lax.fori_loop(1, n, signal, 0)
    return lambda: pl.semaphore_wait(barrier, n - 1)


def remote(source, target, sent, arrived, peer):
    return pltpu.make_async_remote_copy(
        src_ref=source,
        dst_ref=target,
        send_sem=sent,
        recv_sem=arrived,
        device_id={"dp": peer},
        device_id_type=MESH,
    )


class Exchange:
    def __init__(self, n, me, source, target, sent, arrived, same=False):
        self.n, self.me, self.source, self.target = n, me, source, target
        self.sent, self.arrived, self.same = sent, arrived, same

    def copy(self, peer, slot):
        source = self.source if self.same else self.source.at[peer]
        return remote(
            source, self.target.at[slot], self.sent.at[peer], self.arrived.at[slot], peer
        )

    def send(self, peer):
        self.copy(peer, self.me).start()

    def receive(self, peer):
        self.copy(peer, peer).wait_recv()

    def each(self, step_fn):
        def step(k, carry):
            step_fn(lax.rem(self.me + k, self.n))
            return carry

        lax.fori_loop(1, self.n, step, 0)

    def send_all(self):
        self.each(self.send)

    def receive_all(self):
        self.each(lambda peer: self.receive(lax.rem(2 * self.me + self.n - peer, self.n)))

    def finish(self):
        self.each(lambda peer: self.copy(peer, self.me).wait_send())


def mlp_kernel(
    n,
    emb_ref,
    proj_ref,
    gain_ref,
    bias_ref,
    up_bias_ref,
    cot_ref,
    up_hbm,
    down_hbm,
    out_ref,
    columns_ref,
    hidden_ref,
    grad_preact_ref,
    up_bias_grad_ref,
    grad_emb_ref,
    grad_proj_ref,
    sums_ref,
    pairs,
    compressed,
    folded,
    standard,
    standard_ref,
    gain_rows,
    back_ref,
    grad_rows,
    part_send,
    part_recv,
    own_total,
    up_ref,
    down_ref,
    std_in,
    std_rows,
    gh_send,
    gh_recv,
    pre_send,
    pre_recv,
    act_all,
    back_send,
    sums_own,
    out_acc,
    back_acc,
    up_sem,
    down_sem,
    std_ss,
    std_rs,
    gh_ss,
    gh_rs,
    pre_ss,
    pre_rs,
    act_ss,
    act_rs,
    back_ss,
    back_rs,
    sums_ss,
    sums_rs,
    part_ss,
    part_rs,
    total_ss,
    total_rs,
):
    me = lax.axis_index("dp")
    own = emb_ref.shape[0]
    columns_k = proj_ref.shape[1]
    stride = cot_ref.shape[1] // columns_k
    count = n * cot_ref.shape[1]
    rows = cot_ref.shape[0]
    width = up_ref.shape[2]

    def up_copy(j):
        start = pl.multiple_of(j * width, width)
        return pltpu.make_async_copy(up_hbm.at[:, pl.ds(start, width)], up_ref.at[j], up_sem.at[j])

    def down_copy(j):
        start = pl.multiple_of(j * width, width)
        return pltpu.make_async_copy(
            down_hbm.at[pl.ds(start, width), :], down_ref.at[j], down_sem.at[j]
        )

    def loop(step_fn):
        def step(k, carry):
            step_fn(lax.rem(me + k, n))
            return carry

        lax.fori_loop(1, n + 1, step, 0)

    loop(lambda j: down_copy(j).start())
    loop(lambda j: up_copy(j).start())
    await_peers = greet(n, me)

    def whole_sum(values):
        return jnp.sum(jnp.sum(values, axis=1, keepdims=True), axis=0, keepdims=True)

    inv_scales = []
    for b in range(own):
        sample = emb_ref[b]
        pairs[b] = lax.dot_general(
            sample, sample, (((1,), (1,)), ((), ())), preferred_element_type=jnp.float32
        ).astype(jnp.bfloat16)
        compressed[b] = jnp.dot(
            pairs[b], proj_ref[...], preferred_element_type=jnp.float32
        ).astype(jnp.bfloat16)
        interaction = lax.dot_general(
            sample, compressed[b], (((0,), (0,)), ((), ())), preferred_element_type=jnp.float32
        )
        centre = interaction - whole_sum(interaction) / count
        inv_scale = lax.rsqrt(whole_sum(centre * centre) / count + epsilon)
        inv_scales.append(inv_scale)
        folded[b] = centre * inv_scale
        for m in range(0, stride, 2):
            standard[b, :, columns_k * m : columns_k * (m + 2)] = jnp.concatenate(
                [folded[b, pl.ds(m, n, stride=stride), :], folded[b, pl.ds(m + 1, n, stride=stride), :]],
                axis=1,
            )
    for j in range(n):
        standard_ref[j] = standard[:, j, :].astype(jnp.bfloat16)
        gain_rows[j : j + 1, :] = gain_ref[j]
    await_peers()

    std = Exchange(n, me, standard_ref, std_in, std_ss, std_rs)
    gh = Exchange(n, me, gh_send, gh_recv, gh_ss, gh_rs)
    pre = Exchange(n, me, pre_send, pre_recv, pre_ss, pre_rs)
    act = Exchange(n, me, act_all.at[me], act_all, act_ss, act_rs, same=True)
    back = Exchange(n, me, back_send, back_ref, back_ss, back_rs)
    sums = Exchange(n, me, sums_own, sums_ref, sums_ss, sums_rs, same=True)

    std.send_all()
    std_in[me] = standard_ref[me]

    def hidden_step(j):
        down_copy(j).wait()
        part = lax.dot_general(
            cot_ref[...], down_ref[j], (((1,), (1,)), ((), ())), preferred_element_type=jnp.float32
        ).astype(jnp.bfloat16)

        @pl.when(j != me)
        def _():
            gh_send[j] = part
            gh.send(j)

        @pl.when(j == me)
        def _():
            gh_recv[me] = part

    loop(hidden_step)

    std.receive_all()
    for j in range(n):
        std_rows[own * j : own * (j + 1), :] = std_in[j].astype(jnp.float32)
    columns_ref[...] = (std_rows[...] * gain_ref[me] + bias_ref[me]).astype(jnp.bfloat16)

    def preact_step(j):
        up_copy(j).wait()
        part = jnp.dot(
            columns_ref[...], up_ref[j], preferred_element_type=jnp.float32
        ).astype(jnp.bfloat16)

        @pl.when(j != me)
        def _():
            pre_send[j] = part
            pre.send(j)

        @pl.when(j == me)
        def _():
            pre_recv[me] = part

    loop(preact_step)

    gh.receive_all()
    grad_hidden = gh_recv[0].astype(jnp.float32)
    for j in range(1, n):
        grad_hidden = grad_hidden + gh_recv[j].astype(jnp.float32)
    pre.receive_all()
    preact = pre_recv[0].astype(jnp.float32)
    for j in range(1, n):
        preact = preact + pre_recv[j].astype(jnp.float32)
    preact = preact + up_bias_ref[me]
    root = math.sqrt(2 / math.pi)
    square = preact * preact
    bent = jnp.tanh(root * preact * (1.0 + 0.044715 * square))
    half = 0.5 * (1.0 + bent)
    slope = half + 0.5 * preact * (1.0 - bent * bent) * (root * (1.0 + 3 * 0.044715 * square))
    act_all[me, 0] = (preact * half).astype(jnp.bfloat16)
    act_all[me, 1] = (grad_hidden * slope).astype(jnp.bfloat16)
    act.send_all()

    def gather_step(j):
        columns = pl.ds(pl.multiple_of(j * width, width), width)
        hidden = act_all[j, 0]
        grad = act_all[j, 1]
        hidden_ref[:, columns] = hidden
        grad_preact_ref[:, columns] = grad
        up_bias_grad_ref[:, columns] = jnp.sum(grad.astype(jnp.float32), axis=0, keepdims=True)
        out_acc[...] += jnp.dot(hidden, down_ref[j], preferred_element_type=jnp.float32)
        back_acc[...] += lax.dot_general(
            grad, up_ref[j], (((1,), (1,)), ((), ())), preferred_element_type=jnp.float32
        )

    out_acc[...] = jnp.zeros_like(out_acc)
    back_acc[...] = jnp.zeros_like(back_acc)
    gather_step(me)

    def arrive_step(k, carry):
        j = lax.rem(me + n - k, n)
        act.receive(j)
        gather_step(j)
        return carry

    lax.fori_loop(1, n, arrive_step, 0)

    grad_normed = back_acc[...].astype(jnp.bfloat16)
    wide = grad_normed.astype(jnp.float32)
    back_acc[...] = wide
    for j in range(n):
        back_send[j] = back_acc[own * j : own * (j + 1), :].astype(jnp.bfloat16)
    back.send_all()
    back_ref[me] = back_send[me]
    sums_own[0:1, :] = jnp.sum(wide * std_rows[...], axis=0, keepdims=True)
    sums_own[1:2, :] = jnp.sum(wide, axis=0, keepdims=True)
    sums.send_all()
    sums_ref[me] = sums_own[...]
    out_ref[...] = out_acc[...].astype(jnp.bfloat16)
    for exchange in (std, gh, pre, act):
        exchange.finish()
    part = Exchange(n, me, part_send, part_recv, part_ss, part_rs)
    total = Exchange(n, me, own_total, grad_proj_ref, total_ss, total_rs, same=True)
    back.receive_all()
    for j in range(n):
        grad_rows[:, j, :] = back_ref[j].astype(jnp.float32)
    proj_part = None
    saved = []
    for b in range(own):
        scaled = grad_rows[b] * gain_rows[...]
        first = whole_sum(scaled) / count
        second = whole_sum(scaled * standard[b]) / count
        grads = inv_scales[b] * (scaled - first - standard[b] * second)
        for m in range(stride):
            folded[b, pl.ds(m, n, stride=stride), :] = grads[:, columns_k * m : columns_k * (m + 1)]
        grad_matrix = folded[b].astype(jnp.bfloat16)
        grad_compressed = jnp.dot(
            emb_ref[b], grad_matrix, preferred_element_type=jnp.float32
        ).astype(jnp.bfloat16)
        saved.append((grad_matrix, grad_compressed))
        term = jnp.dot(pairs[b], grad_compressed, preferred_element_type=jnp.float32)
        proj_part = term if proj_part is None else proj_part + term
    part_send[...] = proj_part.reshape(part_send.shape)
    part.send_all()
    part_recv[me] = part_send[me]
    for b in range(own):
        grad_matrix, grad_compressed = saved[b]
        last = (((1,), (1,)), ((), ()))
        grad_pairs = lax.dot_general(
            grad_compressed, proj_ref[...], last, preferred_element_type=jnp.float32
        ).astype(jnp.bfloat16)
        turned = lax.dot_general(
            proj_ref[...], grad_compressed, last, preferred_element_type=jnp.float32
        ).astype(jnp.bfloat16)
        grad_sample = lax.dot_general(
            compressed[b], grad_matrix, last, preferred_element_type=jnp.float32
        )
        grad_sample += jnp.dot(grad_pairs, emb_ref[b], preferred_element_type=jnp.float32)
        grad_sample += jnp.dot(turned, emb_ref[b], preferred_element_type=jnp.float32)
        grad_emb_ref[b] = grad_sample.astype(jnp.bfloat16)
        if b == 0:
            part.receive_all()
            whole = part_recv[0]
            for j in range(1, n):
                whole = whole + part_recv[j]
            own_total[...] = whole
            total.send_all()
            grad_proj_ref[me] = whole
    sums.receive_all()
    total.receive_all()
    for exchange in (back, sums, part, total):
        exchange.finish()


def mlp(embeddings, projection, norm_gain, norm_bias, up_weight, up_bias, down_weight, cotangent):
    n = lax.axis_size("dp")
    own, samples, depth = embeddings.shape
    kept = projection.shape[1]
    rows, features = cotangent.shape
    units = up_weight.shape[1]
    width = units // n
    vmem = pl.BlockSpec(memory_space=pltpu.VMEM)
    hbm = pl.BlockSpec(memory_space=pl.ANY)
    bf16, f32 = jnp.bfloat16, jnp.float32
    shape = jax.ShapeDtypeStruct
    return pl.pallas_call(
        functools.partial(mlp_kernel, n),
        out_shape=(
            shape((rows, features), bf16),
            shape((rows, features), bf16),
            shape((rows, units), bf16),
            shape((rows, units), bf16),
            shape((1, units), f32),
            shape(embeddings.shape, bf16),
            shape((n, samples // n, kept), f32),
            shape((n, 2, features), f32),
        ),
        in_specs=[vmem] * 6 + [hbm] * 2,
        out_specs=[vmem] * 8,
        scratch_shapes=[
            pltpu.VMEM((own, samples, samples), bf16),
            pltpu.VMEM((own, samples, kept), bf16),
            pltpu.VMEM((own, depth, kept), f32),
            pltpu.VMEM((own, n, features), f32),
            pltpu.VMEM((n, own, features), bf16),
            pltpu.VMEM((n, features), f32),
            pltpu.VMEM((n, own, features), bf16),
            pltpu.VMEM((own, n, features), f32),
            pltpu.VMEM((n, samples // n, kept), f32),
            pltpu.VMEM((n, samples // n, kept), f32),
            pltpu.VMEM((samples // n, kept), f32),
            pltpu.VMEM((n, features, width), bf16),
            pltpu.VMEM((n, width, features), bf16),
            pltpu.VMEM((n, own, features), bf16),
            pltpu.VMEM((rows, features), f32),
            pltpu.VMEM((n, rows, width), bf16),
            pltpu.VMEM((n, rows, width), bf16),
            pltpu.VMEM((n, rows, width), bf16),
            pltpu.VMEM((n, rows, width), bf16),
            pltpu.VMEM((n, 2, rows, width), bf16),
            pltpu.VMEM((n, own, features), bf16),
            pltpu.VMEM((2, features), f32),
            pltpu.VMEM((rows, features), f32),
            pltpu.VMEM((rows, features), f32),
        ]
        + [pltpu.SemaphoreType.DMA((n,))] * 18,
        compiler_params=pltpu.CompilerParams(
            collective_id=0, has_side_effects=True, vmem_limit_bytes=48 * 2**20
        ),
        cost_estimate=pl.CostEstimate(
            flops=8 * rows * features * units,
            bytes_accessed=4 * features * units,
            transcendentals=rows * width,
        ),
        name="perceptron",
    )(
        embeddings,
        projection,
        norm_gain.reshape(n, 1, features),
        norm_bias.reshape(n, 1, features),
        up_bias.reshape(n, 1, width),
        cotangent,
        up_weight,
        down_weight,
    )


def weight_kernel(columns_ref, grad_preact_ref, hidden_ref, cot_ref, up_ref, down_ref):
    up_ref[...] = contract_rows(columns_ref[...], grad_preact_ref[...])
    down_ref[...] = contract_rows(hidden_ref[...], cot_ref[...])


def weight_grads(columns, grad_preact, hidden, cotangent):
    rows, features = columns.shape
    units = hidden.shape[1]
    steps = math.gcd(features, units) // 128
    while steps > 16:
        steps //= 2

    def part(extent):
        return pl.BlockSpec((rows, extent // steps), lambda i: (0, i))

    def whole(extent):
        return pl.BlockSpec((rows, extent), lambda i: (0, 0))

    def result(height, width):
        return pl.BlockSpec((height // steps, width), lambda i: (i, 0))

    return pl.pallas_call(
        weight_kernel,
        grid=(steps,),
        out_shape=(
            jax.ShapeDtypeStruct((features, units), jnp.float32),
            jax.ShapeDtypeStruct((units, features), jnp.float32),
        ),
        in_specs=[part(features), whole(units), part(units), whole(features)],
        out_specs=(result(features, units), result(units, features)),
        compiler_params=pltpu.CompilerParams(vmem_limit_bytes=40 * 2**20),
        name="weight_grads",
    )(columns, grad_preact, hidden, cotangent)


def body(embeddings, projection, norm_gain, norm_bias, up_weight, up_bias, down_weight, cotangent):
    n = lax.axis_size("dp")
    own_rows = embeddings.shape[0]
    if (up_weight.shape[1] // n) % 128 or cotangent.shape[0] % 16:
        return plain_body(
            embeddings, projection, norm_gain, norm_bias, up_weight, up_bias, down_weight, cotangent
        )
    out, columns, hidden, grad_preact, grad_up_bias, grad_embeddings, grad_projection, sums = mlp(
        embeddings, projection, norm_gain, norm_bias, up_weight, up_bias, down_weight, cotangent
    )
    grad_up, grad_down = weight_grads(columns, grad_preact, hidden, cotangent)
    return (
        out,
        grad_embeddings,
        grad_projection.reshape(projection.shape),
        sums[:, 0, :].reshape(-1),
        sums[:, 1, :].reshape(-1),
        grad_up,
        grad_up_bias.reshape(-1),
        grad_down,
    )


def solution(mesh):
    return jax.shard_map(
        body,
        mesh=mesh,
        in_specs=(
            P(("groups", "dp"), None, None),
            P(),
            P(),
            P(),
            P("dp", None),
            P(),
            P(None, "dp"),
            P("groups", "dp"),
        ),
        out_specs=(
            P("groups", "dp"),
            P(("groups", "dp"), None, None),
            P("groups", None),
            P("groups"),
            P("groups"),
            P(("groups", "dp"), None),
            P("groups"),
            P("groups", "dp"),
        ),
        check_vma=False,
    )
```

```python
import functools
import math

import jax
import jax.numpy as jnp
from jax import lax
from jax.experimental import pallas as pl
from jax.experimental.pallas import tpu as pltpu
from jax.sharding import PartitionSpec as P

epsilon = 1e-05


def activate(values):
    return jax.nn.gelu(values, approximate=True)


def activate_back(preact, grad_hidden):
    _, pullback = jax.vjp(activate, preact)
    return pullback(grad_hidden)[0]


def interact_row(sample, projection):
    pair_dots = jnp.dot(sample, sample.T, preferred_element_type=jnp.float32).astype(jnp.bfloat16)
    compressed = jnp.dot(pair_dots, projection, preferred_element_type=jnp.float32).astype(
        jnp.bfloat16
    )
    interaction = jnp.dot(sample.T, compressed, preferred_element_type=jnp.float32)
    return interaction.reshape(-1)


def interact_back(sample, projection, grad_flat):
    pair_dots = jnp.dot(sample, sample.T, preferred_element_type=jnp.float32).astype(jnp.bfloat16)
    compressed = jnp.dot(pair_dots, projection, preferred_element_type=jnp.float32).astype(
        jnp.bfloat16
    )
    grad_matrix = grad_flat.reshape(sample.shape[1], projection.shape[1])
    grad_compressed = jnp.dot(sample, grad_matrix, preferred_element_type=jnp.float32).astype(
        jnp.bfloat16
    )
    grad_direct = jnp.dot(compressed, grad_matrix.T, preferred_element_type=jnp.float32)
    grad_pairs = jnp.dot(grad_compressed, projection.T, preferred_element_type=jnp.float32).astype(
        jnp.bfloat16
    )
    grad_sample = grad_direct + jnp.dot(grad_pairs, sample, preferred_element_type=jnp.float32)
    grad_sample = grad_sample + jnp.dot(grad_pairs.T, sample, preferred_element_type=jnp.float32)
    grad_proj = jnp.dot(pair_dots.T, grad_compressed, preferred_element_type=jnp.float32)
    return (grad_sample.astype(jnp.bfloat16), grad_proj)


def layer_norm(interaction):
    centre = interaction - jnp.mean(interaction, axis=-1, keepdims=True)
    variance = jnp.mean(centre * centre, axis=-1, keepdims=True)
    inv_scale = lax.rsqrt(variance + epsilon)
    return (centre * inv_scale, inv_scale)


def norm_back(grad_normed, standard, inv_scale, norm_gain):
    scaled = grad_normed * norm_gain
    first = jnp.mean(scaled, axis=-1, keepdims=True)
    second = jnp.mean(scaled * standard, axis=-1, keepdims=True)
    return inv_scale * (scaled - first - standard * second)


def sum_rows(term, own_rows):
    return lax.psum_scatter(
        term(jnp.int32(0), lax.axis_size("dp") * own_rows), "dp", scatter_dimension=0, tiled=True
    )


def fold_rows(values, step_fn, initial):
    return step_fn(initial, lax.all_gather(values, "dp", axis=0, tiled=True), jnp.int32(0))


def contract_rows(left, right):
    return lax.dot_general(
        left, right, (((0,), (0,)), ((), ())), preferred_element_type=jnp.float32
    )


def contract_last(left, right):
    return lax.dot_general(
        left, right, (((1,), (1,)), ((), ())), preferred_element_type=jnp.float32
    )


def plain_body(embeddings, projection, norm_gain, norm_bias, up_weight, up_bias, down_weight, cotangent):
    own_rows = embeddings.shape[0]
    interaction = jax.vmap(lambda sample: interact_row(sample, projection))(embeddings)
    standard, inv_scale = layer_norm(interaction)
    normed = (standard * norm_gain + norm_bias).astype(jnp.bfloat16)
    columns = lax.all_to_all(normed, "dp", split_axis=1, concat_axis=0, tiled=True)
    all_rows = columns.shape[0]
    own_features = up_weight.shape[0]
    hidden_units = up_weight.shape[1]

    def preact_term(offset, amount):
        return jnp.dot(columns, up_weight, preferred_element_type=jnp.float32)

    preact = sum_rows(preact_term, own_rows) + up_bias
    hidden = activate(preact).astype(jnp.bfloat16)

    def output_step(running, block_rows, offset):
        product = jnp.dot(block_rows, down_weight, preferred_element_type=jnp.float32)
        down_acc = contract_rows(block_rows, cotangent)
        return (product, down_acc)

    start_state = (
        jnp.zeros((all_rows, down_weight.shape[1]), jnp.float32),
        jnp.zeros(down_weight.shape, jnp.float32),
    )
    out_columns, grad_down = fold_rows(hidden, output_step, start_state)

    def hidden_term(offset, amount):
        return contract_last(cotangent, down_weight)

    grad_hidden = sum_rows(hidden_term, own_rows)
    grad_preact = activate_back(preact, grad_hidden).astype(jnp.bfloat16)

    def gradient_step(running, block_rows, offset):
        product = contract_last(block_rows, up_weight)
        up_acc = contract_rows(columns, block_rows)
        bias_acc = jnp.sum(block_rows.astype(jnp.float32), axis=0)
        return (product, up_acc, bias_acc)

    start_grad = (
        jnp.zeros((all_rows, own_features), jnp.float32),
        jnp.zeros(up_weight.shape, jnp.float32),
        jnp.zeros((hidden_units,), jnp.float32),
    )
    back_columns, grad_up, grad_up_bias = fold_rows(grad_preact, gradient_step, start_grad)
    grad_normed = lax.all_to_all(
        back_columns.astype(jnp.bfloat16), "dp", split_axis=0, concat_axis=1, tiled=True
    ).astype(jnp.float32)
    gain_part = jnp.sum(grad_normed * standard, axis=0)
    bias_part = jnp.sum(grad_normed, axis=0)
    grad_interaction = norm_back(grad_normed, standard, inv_scale, norm_gain).astype(jnp.bfloat16)
    grad_embeddings, proj_rows = jax.vmap(
        lambda sample, grad_flat: interact_back(sample, projection, grad_flat)
    )(embeddings, grad_interaction)
    proj_part = jnp.sum(proj_rows, axis=0)
    grad_projection, grad_gain, grad_bias = lax.psum((proj_part, gain_part, bias_part), "dp")
    return (
        out_columns.astype(jnp.bfloat16),
        grad_embeddings,
        grad_projection,
        grad_gain,
        grad_bias,
        grad_up,
        grad_up_bias,
        grad_down,
    )


MESH = pl.DeviceIdType.MESH


def greet(n, me):
    barrier = pltpu.get_barrier_semaphore()

    def signal(step, carry):
        peer = lax.rem(me + step, n)
        pl.semaphore_signal(barrier, inc=1, device_id={"dp": peer}, device_id_type=MESH)
        return carry

    lax.fori_loop(1, n, signal, 0)
    return lambda: pl.semaphore_wait(barrier, n - 1)


def remote(source, target, sent, arrived, peer):
    return pltpu.make_async_remote_copy(
        src_ref=source,
        dst_ref=target,
        send_sem=sent,
        recv_sem=arrived,
        device_id={"dp": peer},
        device_id_type=MESH,
    )


class Exchange:
    def __init__(self, n, me, source, target, sent, arrived, same=False):
        self.n, self.me, self.source, self.target = n, me, source, target
        self.sent, self.arrived, self.same = sent, arrived, same

    def copy(self, peer, slot):
        source = self.source if self.same else self.source.at[peer]
        return remote(
            source, self.target.at[slot], self.sent.at[peer], self.arrived.at[slot], peer
        )

    def send(self, peer):
        self.copy(peer, self.me).start()

    def receive(self, peer):
        self.copy(peer, peer).wait_recv()

    def each(self, step_fn):
        def step(k, carry):
            step_fn(lax.rem(self.me + k, self.n))
            return carry

        lax.fori_loop(1, self.n, step, 0)

    def send_all(self):
        self.each(self.send)

    def receive_all(self):
        self.each(lambda peer: self.receive(lax.rem(2 * self.me + self.n - peer, self.n)))

    def finish(self):
        self.each(lambda peer: self.copy(peer, self.me).wait_send())


def mlp_kernel(
    n,
    proj_ref,
    emb_hbm,
    gain_hbm,
    bias_hbm,
    up_bias_hbm,
    cot_hbm,
    up_hbm,
    down_hbm,
    out_ref,
    columns_ref,
    hidden_ref,
    grad_preact_ref,
    up_bias_grad_ref,
    grad_emb_ref,
    grad_proj_ref,
    sums_ref,
    emb_ref,
    gain_ref,
    bias_ref,
    up_bias_ref,
    cot_ref,
    pairs,
    compressed,
    folded,
    standard,
    standard_ref,
    gain_rows,
    back_ref,
    grad_rows,
    part_send,
    part_recv,
    own_total,
    up_ref,
    down_ref,
    std_in,
    std_rows,
    gh_pair_send,
    gh_pair_recv,
    gh_send,
    gh_recv,
    pre_pair_send,
    pre_pair_recv,
    pre_send,
    pre_recv,
    act_all,
    back_send,
    sums_own,
    out_acc,
    back_acc,
    up_sem,
    down_sem,
    std_ss,
    std_rs,
    gh_pair_ss,
    gh_pair_rs,
    gh_ss,
    gh_rs,
    pre_pair_ss,
    pre_pair_rs,
    pre_ss,
    pre_rs,
    pass_ss,
    small_sem,
    act_ss,
    act_rs,
    back_ss,
    back_rs,
    sums_ss,
    sums_rs,
    part_ss,
    part_rs,
    total_ss,
    total_rs,
):
    me = lax.axis_index("dp")
    own = emb_ref.shape[0]
    columns_k = proj_ref.shape[1]
    stride = cot_ref.shape[1] // columns_k
    count = n * cot_ref.shape[1]
    rows = cot_ref.shape[0]
    width = up_ref.shape[2]

    def up_copy(j):
        start = pl.multiple_of(j * width, width)
        return pltpu.make_async_copy(up_hbm.at[:, pl.ds(start, width)], up_ref.at[j], up_sem.at[j])

    def down_copy(j):
        start = pl.multiple_of(j * width, width)
        return pltpu.make_async_copy(
            down_hbm.at[pl.ds(start, width), :], down_ref.at[j], down_sem.at[j]
        )

    half_n = n // 2
    core = lax.rem(me, 2)
    place = me // 2
    sibling = me + 1 - 2 * core

    def places(step_fn):
        def step(k, carry):
            step_fn(lax.rem(place + k, half_n))
            return carry

        lax.fori_loop(1, half_n + 1, step, 0)

    def other_places(step_fn):
        def step(k, carry):
            step_fn(lax.rem(place + k, half_n))
            return carry

        lax.fori_loop(1, half_n, step, 0)

    small = [
        pltpu.make_async_copy(source, target, small_sem.at[i])
        for i, (source, target) in enumerate(
            (
                (emb_hbm, emb_ref),
                (cot_hbm, cot_ref),
                (gain_hbm, gain_ref),
                (bias_hbm.at[me], bias_ref),
                (up_bias_hbm.at[me], up_bias_ref),
            )
        )
    ]
    for copy in small:
        copy.start()
    places(lambda p: down_copy(2 * p + 1 - core).start())
    places(lambda p: down_copy(2 * p + core).start())
    places(lambda p: up_copy(2 * p + 1 - core).start())
    places(lambda p: up_copy(2 * p + core).start())
    await_peers = greet(n, me)

    def whole_sum(values):
        return jnp.sum(jnp.sum(values, axis=1, keepdims=True), axis=0, keepdims=True)

    for copy in small:
        copy.wait()
    inv_scales = []
    for b in range(own):
        sample = emb_ref[b]
        pairs[b] = lax.dot_general(
            sample, sample, (((1,), (1,)), ((), ())), preferred_element_type=jnp.float32
        ).astype(jnp.bfloat16)
        compressed[b] = jnp.dot(
            pairs[b], proj_ref[...], preferred_element_type=jnp.float32
        ).astype(jnp.bfloat16)
        interaction = lax.dot_general(
            sample, compressed[b], (((0,), (0,)), ((), ())), preferred_element_type=jnp.float32
        )
        centre = interaction - whole_sum(interaction) / count
        inv_scale = lax.rsqrt(whole_sum(centre * centre) / count + epsilon)
        inv_scales.append(inv_scale)
        folded[b] = centre * inv_scale
        for m in range(0, stride, 2):
            standard[b, :, columns_k * m : columns_k * (m + 2)] = jnp.concatenate(
                [folded[b, pl.ds(m, n, stride=stride), :], folded[b, pl.ds(m + 1, n, stride=stride), :]],
                axis=1,
            )
    for j in range(n):
        standard_ref[j] = standard[:, j, :].astype(jnp.bfloat16)
        gain_rows[j : j + 1, :] = gain_ref[j]
    await_peers()

    std = Exchange(n, me, standard_ref, std_in, std_ss, std_rs)

    def reduce_blocks(part_fn, pair_send, pair_recv, send, recv, pair_ss, pair_rs, ss, rs):
        def to_sibling(p):
            return remote(
                pair_send.at[p], pair_recv.at[p], pair_ss.at[p], pair_rs.at[p], sibling
            )

        def to_owner(p):
            return remote(send.at[p], recv.at[place], ss.at[p], rs.at[place], 2 * p + core)

        def from_place(p):
            return remote(send.at[p], recv.at[p], ss.at[p], rs.at[p], 2 * p + core)

        def first(p):
            pair_send[p] = part_fn(2 * p + 1 - core).astype(jnp.bfloat16)
            to_sibling(p).start()

        def second(p):
            part = part_fn(2 * p + core)
            to_sibling(p).wait_recv()
            part = (part + pair_recv[p].astype(jnp.float32)).astype(jnp.bfloat16)

            @pl.when(p != place)
            def _():
                send[p] = part
                to_owner(p).start()

            @pl.when(p == place)
            def _():
                recv[place] = part

        places(first)
        places(second)

        def result():
            other_places(lambda p: from_place(p).wait_recv())
            total = recv[0].astype(jnp.float32)
            for p in range(1, half_n):
                total = total + recv[p].astype(jnp.float32)
            return total

        def finish():
            places(lambda p: to_sibling(p).wait_send())
            other_places(lambda p: to_owner(p).wait_send())

        return result, finish

    back = Exchange(n, me, back_send, back_ref, back_ss, back_rs)
    sums = Exchange(n, me, sums_own, sums_ref, sums_ss, sums_rs, same=True)

    std.send_all()
    std_in[me] = standard_ref[me]

    def hidden_part(j):
        down_copy(j).wait()
        return lax.dot_general(
            cot_ref[...], down_ref[j], (((1,), (1,)), ((), ())), preferred_element_type=jnp.float32
        )

    gh_result, gh_finish = reduce_blocks(
        hidden_part,
        gh_pair_send,
        gh_pair_recv,
        gh_send,
        gh_recv,
        gh_pair_ss,
        gh_pair_rs,
        gh_ss,
        gh_rs,
    )

    std.receive_all()
    for j in range(n):
        std_rows[own * j : own * (j + 1), :] = std_in[j].astype(jnp.float32)
    columns_ref[...] = (std_rows[...] * gain_ref[me] + bias_ref[...]).astype(jnp.bfloat16)

    def preact_part(j):
        up_copy(j).wait()
        return jnp.dot(columns_ref[...], up_ref[j], preferred_element_type=jnp.float32)

    pre_result, pre_finish = reduce_blocks(
        preact_part,
        pre_pair_send,
        pre_pair_recv,
        pre_send,
        pre_recv,
        pre_pair_ss,
        pre_pair_rs,
        pre_ss,
        pre_rs,
    )
    grad_hidden = gh_result()
    preact = pre_result() + up_bias_ref[...]
    root = math.sqrt(2 / math.pi)
    square = preact * preact
    bent = jnp.tanh(root * preact * (1.0 + 0.044715 * square))
    half = 0.5 * (1.0 + bent)
    slope = half + 0.5 * preact * (1.0 - bent * bent) * (root * (1.0 + 3 * 0.044715 * square))
    act_all[me, 0] = (preact * half).astype(jnp.bfloat16)
    act_all[me, 1] = (grad_hidden * slope).astype(jnp.bfloat16)

    def act_copy(j, peer, sent):
        return remote(act_all.at[j], act_all.at[j], sent, act_rs.at[j], peer)

    act_copy(me, sibling, act_ss.at[sibling]).start()
    other_places(lambda p: act_copy(me, 2 * p + core, act_ss.at[2 * p + core]).start())

    def gather_step(j):
        columns = pl.ds(pl.multiple_of(j * width, width), width)
        hidden = act_all[j, 0]
        grad = act_all[j, 1]
        hidden_ref[:, columns] = hidden
        grad_preact_ref[:, columns] = grad
        up_bias_grad_ref[:, columns] = jnp.sum(grad.astype(jnp.float32), axis=0, keepdims=True)
        out_acc[...] += jnp.dot(hidden, down_ref[j], preferred_element_type=jnp.float32)
        back_acc[...] += lax.dot_general(
            grad, up_ref[j], (((1,), (1,)), ((), ())), preferred_element_type=jnp.float32
        )

    out_acc[...] = jnp.zeros_like(out_acc)
    back_acc[...] = jnp.zeros_like(back_acc)
    gather_step(me)

    act_copy(sibling, sibling, act_ss.at[sibling]).wait_recv()
    gather_step(sibling)

    def arrive_step(k, carry):
        p = lax.rem(place + half_n - k, half_n)
        near = 2 * p + core
        far = 2 * p + 1 - core
        act_copy(near, sibling, act_ss.at[near]).wait_recv()
        act_copy(near, sibling, pass_ss.at[near]).start()
        gather_step(near)
        act_copy(far, sibling, act_ss.at[far]).wait_recv()
        gather_step(far)
        return carry

    lax.fori_loop(1, half_n, arrive_step, 0)

    grad_normed = back_acc[...].astype(jnp.bfloat16)
    wide = grad_normed.astype(jnp.float32)
    back_acc[...] = wide
    for j in range(n):
        back_send[j] = back_acc[own * j : own * (j + 1), :].astype(jnp.bfloat16)
    back.send_all()
    back_ref[me] = back_send[me]
    sums_own[0:1, :] = jnp.sum(wide * std_rows[...], axis=0, keepdims=True)
    sums_own[1:2, :] = jnp.sum(wide, axis=0, keepdims=True)
    sums.send_all()
    sums_ref[me] = sums_own[...]
    out_ref[...] = out_acc[...].astype(jnp.bfloat16)
    std.finish()
    gh_finish()
    pre_finish()
    act_copy(me, sibling, act_ss.at[sibling]).wait_send()
    other_places(lambda p: act_copy(me, 2 * p + core, act_ss.at[2 * p + core]).wait_send())
    other_places(lambda p: act_copy(2 * p + core, sibling, pass_ss.at[2 * p + core]).wait_send())
    part = Exchange(n, me, part_send, part_recv, part_ss, part_rs)
    total = Exchange(n, me, own_total, grad_proj_ref, total_ss, total_rs, same=True)
    back.receive_all()
    for j in range(n):
        grad_rows[:, j, :] = back_ref[j].astype(jnp.float32)
    proj_part = None
    saved = []
    for b in range(own):
        scaled = grad_rows[b] * gain_rows[...]
        first = whole_sum(scaled) / count
        second = whole_sum(scaled * standard[b]) / count
        grads = inv_scales[b] * (scaled - first - standard[b] * second)
        for m in range(stride):
            folded[b, pl.ds(m, n, stride=stride), :] = grads[:, columns_k * m : columns_k * (m + 1)]
        grad_matrix = folded[b].astype(jnp.bfloat16)
        grad_compressed = jnp.dot(
            emb_ref[b], grad_matrix, preferred_element_type=jnp.float32
        ).astype(jnp.bfloat16)
        saved.append((grad_matrix, grad_compressed))
        term = jnp.dot(pairs[b], grad_compressed, preferred_element_type=jnp.float32)
        proj_part = term if proj_part is None else proj_part + term
    part_send[...] = proj_part.reshape(part_send.shape)
    part.send_all()
    part_recv[me] = part_send[me]
    for b in range(own):
        grad_matrix, grad_compressed = saved[b]
        last = (((1,), (1,)), ((), ()))
        grad_pairs = lax.dot_general(
            grad_compressed, proj_ref[...], last, preferred_element_type=jnp.float32
        ).astype(jnp.bfloat16)
        turned = lax.dot_general(
            proj_ref[...], grad_compressed, last, preferred_element_type=jnp.float32
        ).astype(jnp.bfloat16)
        grad_sample = lax.dot_general(
            compressed[b], grad_matrix, last, preferred_element_type=jnp.float32
        )
        grad_sample += jnp.dot(grad_pairs, emb_ref[b], preferred_element_type=jnp.float32)
        grad_sample += jnp.dot(turned, emb_ref[b], preferred_element_type=jnp.float32)
        grad_emb_ref[b] = grad_sample.astype(jnp.bfloat16)
        if b == 0:
            part.receive_all()
            whole = part_recv[0]
            for j in range(1, n):
                whole = whole + part_recv[j]
            own_total[...] = whole
            total.send_all()
            grad_proj_ref[me] = whole
    sums.receive_all()
    total.receive_all()
    for exchange in (back, sums, part, total):
        exchange.finish()


def mlp(embeddings, projection, norm_gain, norm_bias, up_weight, up_bias, down_weight, cotangent):
    n = lax.axis_size("dp")
    own, samples, depth = embeddings.shape
    kept = projection.shape[1]
    rows, features = cotangent.shape
    units = up_weight.shape[1]
    width = units // n
    vmem = pl.BlockSpec(memory_space=pltpu.VMEM)
    hbm = pl.BlockSpec(memory_space=pl.ANY)
    bf16, f32 = jnp.bfloat16, jnp.float32
    shape = jax.ShapeDtypeStruct
    return pl.pallas_call(
        functools.partial(mlp_kernel, n),
        out_shape=(
            shape((rows, features), bf16),
            shape((rows, features), bf16),
            shape((rows, units), bf16),
            shape((rows, units), bf16),
            shape((1, units), f32),
            shape(embeddings.shape, bf16),
            shape((n, samples // n, kept), f32),
            shape((n, 2, features), f32),
        ),
        in_specs=[vmem] + [hbm] * 7,
        out_specs=[vmem] * 8,
        scratch_shapes=[
            pltpu.VMEM(embeddings.shape, bf16),
            pltpu.VMEM((n, 1, features), f32),
            pltpu.VMEM((1, features), f32),
            pltpu.VMEM((1, width), f32),
            pltpu.VMEM((rows, features), bf16),
            pltpu.VMEM((own, samples, samples), bf16),
            pltpu.VMEM((own, samples, kept), bf16),
            pltpu.VMEM((own, depth, kept), f32),
            pltpu.VMEM((own, n, features), f32),
            pltpu.VMEM((n, own, features), bf16),
            pltpu.VMEM((n, features), f32),
            pltpu.VMEM((n, own, features), bf16),
            pltpu.VMEM((own, n, features), f32),
            pltpu.VMEM((n, samples // n, kept), f32),
            pltpu.VMEM((n, samples // n, kept), f32),
            pltpu.VMEM((samples // n, kept), f32),
            pltpu.VMEM((n, features, width), bf16),
            pltpu.VMEM((n, width, features), bf16),
            pltpu.VMEM((n, own, features), bf16),
            pltpu.VMEM((rows, features), f32),
        ]
        + [pltpu.VMEM((n // 2, rows, width), bf16)] * 8
        + [
            pltpu.VMEM((n, 2, rows, width), bf16),
            pltpu.VMEM((n, own, features), bf16),
            pltpu.VMEM((2, features), f32),
            pltpu.VMEM((rows, features), f32),
            pltpu.VMEM((rows, features), f32),
        ]
        + [pltpu.SemaphoreType.DMA((n,))] * 24,
        compiler_params=pltpu.CompilerParams(
            collective_id=0, has_side_effects=True, vmem_limit_bytes=48 * 2**20
        ),
        cost_estimate=pl.CostEstimate(
            flops=8 * rows * features * units,
            bytes_accessed=4 * features * units,
            transcendentals=rows * width,
        ),
        name="perceptron",
    )(
        projection,
        embeddings,
        norm_gain.reshape(n, 1, features),
        norm_bias.reshape(n, 1, features),
        up_bias.reshape(n, 1, width),
        cotangent,
        up_weight,
        down_weight,
    )


def weight_kernel(
    columns_ref,
    grad_preact_ref,
    hidden_ref,
    cot_ref,
    out_in,
    emb_in,
    sums_in,
    up_ref,
    down_ref,
    out_ref,
    emb_ref,
    gain_ref,
    bias_ref,
):
    up_ref[...] = contract_rows(columns_ref[...], grad_preact_ref[...])
    down_ref[...] = contract_rows(hidden_ref[...], cot_ref[...])
    out_ref[...] = out_in[...]
    emb_ref[...] = emb_in[...]
    gain_ref[...] = sums_in[:, 0:1, :]
    bias_ref[...] = sums_in[:, 1:2, :]


def finish_grads(columns, grad_preact, hidden, cotangent, out, grad_embeddings, sums):
    rows, features = columns.shape
    units = hidden.shape[1]
    own, samples, depth = grad_embeddings.shape
    n = sums.shape[0]
    steps = math.gcd(math.gcd(features, units) // 128, math.gcd(n, samples // 16))

    def part(extent):
        return pl.BlockSpec((rows, extent // steps), lambda i: (0, i))

    def whole(extent):
        return pl.BlockSpec((rows, extent), lambda i: (0, 0))

    def result(height, width):
        return pl.BlockSpec((height // steps, width), lambda i: (i, 0))

    def lead(second):
        return pl.BlockSpec((n // steps, second, features), lambda i: (i, 0, 0))

    emb = pl.BlockSpec((own, samples // steps, depth), lambda i: (0, i, 0))
    shape = jax.ShapeDtypeStruct
    return pl.pallas_call(
        weight_kernel,
        grid=(steps,),
        out_shape=(
            shape((features, units), jnp.float32),
            shape((units, features), jnp.float32),
            shape(out.shape, out.dtype),
            shape(grad_embeddings.shape, grad_embeddings.dtype),
            shape((n, 1, features), jnp.float32),
            shape((n, 1, features), jnp.float32),
        ),
        in_specs=[
            part(features),
            whole(units),
            part(units),
            whole(features),
            part(features),
            emb,
            lead(2),
        ],
        out_specs=(
            result(features, units),
            result(units, features),
            part(features),
            emb,
            lead(1),
            lead(1),
        ),
        compiler_params=pltpu.CompilerParams(vmem_limit_bytes=40 * 2**20),
        name="weight_grads",
    )(columns, grad_preact, hidden, cotangent, out, grad_embeddings, sums)


def body(embeddings, projection, norm_gain, norm_bias, up_weight, up_bias, down_weight, cotangent):
    n = lax.axis_size("dp")
    own_rows = embeddings.shape[0]
    if n % 2 or (up_weight.shape[1] // n) % 128 or cotangent.shape[0] % 16:
        return plain_body(
            embeddings, projection, norm_gain, norm_bias, up_weight, up_bias, down_weight, cotangent
        )
    out, columns, hidden, grad_preact, grad_up_bias, grad_embeddings, grad_projection, sums = mlp(
        embeddings, projection, norm_gain, norm_bias, up_weight, up_bias, down_weight, cotangent
    )
    grad_up, grad_down, out, grad_embeddings, grad_gain, grad_bias = finish_grads(
        columns, grad_preact, hidden, cotangent, out, grad_embeddings, sums
    )
    return (
        out,
        grad_embeddings,
        grad_projection.reshape(projection.shape),
        grad_gain.reshape(-1),
        grad_bias.reshape(-1),
        grad_up,
        grad_up_bias.reshape(-1),
        grad_down,
    )


def solution(mesh):
    return jax.shard_map(
        body,
        mesh=mesh,
        in_specs=(
            P(("groups", "dp"), None, None),
            P(),
            P(),
            P(),
            P("dp", None),
            P(),
            P(None, "dp"),
            P("groups", "dp"),
        ),
        out_specs=(
            P("groups", "dp"),
            P(("groups", "dp"), None, None),
            P("groups", None),
            P("groups"),
            P("groups"),
            P(("groups", "dp"), None),
            P("groups"),
            P("groups", "dp"),
        ),
        check_vma=False,
    )
```
